768 devices in a mesh: row: 16 (over y, core), col: 48 (over z, x).
Axes of the slice: x: 4, y: 8, z: 12, core: 2. Of those that a mesh axis runs over, the one named last changes fastest.
Arguments:
- three_centre: bfloat16 [64, 2048, 12288], P(None, 'row', 'col'), may hold values from -6 to 6
- block_mask: int32 [1, 32, 192], P(None, 'row', 'col'), may hold values 0 or 1
- g_occ: bfloat16 [12288, 192], P('col'), may hold values from -0.1875 to 0.1875
- g_virt: bfloat16 [2048, 2048], P('row'), may hold values from -0.125 to 0.125
Outputs:
- contracted: bfloat16 [192, 64, 2048], P('col', None, 'row')
The draws below stay inside these ranges and needn't reach their ends.
All inputs are finite; a program needn't handle non-finite values. No bound on the sum of `block_mask` on one device may be relied on, other than what follows from the above.
Results may differ from the reference program's by a relative error of at most 0.0049.
Values may be sent and summed in bfloat16 or wider, within the bound.
A program may use at most 32 MiB of HBM per device.

```python
import jax
import jax.numpy as jnp
from jax import lax

BS = 64
PB = 1
MB_DEV = 2
NB_DEV = 4
NP = 64
NMU = 2048
NNU = 12288
NSIG = 192
N_ROW = 16
N_COL = 48


def touch_ends(drawn, own_key, smallest, high):
    index_at = [jax.random.randint(jax.random.fold_in(own_key, axis), (), 0, length) for axis, length in enumerate(drawn.shape)]
    widest = drawn.shape.index(max(drawn.shape))
    neighbour = index_at[:widest] + [(index_at[widest] + 1) % drawn.shape[widest]] + index_at[widest + 1:]
    return drawn.at[tuple(index_at)].set(smallest).at[tuple(neighbour)].set(high)


def spiked(array, rng, source, target, blocks, factor):
    def block_of(position):
        return (jnp.arange(array.shape[position]) // (array.shape[position] // blocks)).reshape((-1,) + (1,) * (array.ndim - 1 - position))

    near = jax.random.permutation(rng, blocks)[block_of(target)]
    far = (block_of(target) + blocks // 2) % blocks
    return jnp.where((block_of(source) == near) | (block_of(source) == far), factor * array, array)


def levels(stream_key, dims, cuts, least, largest):
    level, own = 1.0, jax.random.fold_in(stream_key, 6)
    for axis_at, shards_of in cuts:
        steps = jnp.exp(jax.random.uniform(jax.random.fold_in(own, axis_at), (shards_of,), jnp.float32, least / len(cuts), largest / len(cuts)))
        level = level * jnp.repeat(steps, dims[axis_at] // shards_of).reshape([-1 if axis == axis_at else 1 for axis in range(len(dims))])
    return level


def normal_values(own_key, dims, spread, bound, split=(), kind=jnp.bfloat16):
    values = spread * jax.random.normal(own_key, dims, jnp.float32)
    if split:
        values = values * levels(own_key, dims, split, -0.22, 0.18)
    return jnp.clip(values, -bound, bound).astype(kind)


def bell_draw_with(rng, shape, spread, limit, split, heavy, kind=jnp.bfloat16):
    drawn = spread * jax.random.normal(rng, shape, jnp.float32)
    if split:
        drawn = drawn * levels(rng, shape, split, -0.22, 0.18)
    return jnp.clip(spiked(drawn, jax.random.fold_in(rng, 3), *heavy), -limit, limit).astype(kind)


def setup_inputs(seed: int = 0) -> dict:
    arg_keys = jax.random.split(jax.random.key(seed), 5)
    return {
        "three_centre": normal_values(arg_keys[0], (NP, NMU, NNU), 1.0, 6.0, ((1, 16), (2, 48))),
        "block_mask": touch_ends((jax.random.randint(arg_keys[1], (PB, MB_DEV * N_ROW, NB_DEV * N_COL), 0, 2) < 1).astype(jnp.int32), jax.random.fold_in(arg_keys[1], 1), 0, 1),
        "g_occ": bell_draw_with(arg_keys[2], (NNU, NSIG), (NNU // 2) ** -0.5, 0.1875, ((0, 48),), (0, 1, 48, 3.25)),
        "g_virt": normal_values(arg_keys[3], (NMU, NMU), NMU ** -0.5, 0.125, ((0, 16),)),
    }


def expand_mask(mask_blocks, block_size):
    ri_blocks, mu_blocks, nu_blocks = mask_blocks.shape
    expanded = mask_blocks.astype(jnp.float32)[:, None, :, None, :, None]
    expanded = jnp.broadcast_to(expanded, (ri_blocks, block_size, mu_blocks, block_size, nu_blocks, block_size))
    return expanded.reshape(ri_blocks * block_size, mu_blocks * block_size, nu_blocks * block_size)


def reference(three_centre, block_mask, g_occ, g_virt):
    width = NB_DEV * BS

    def accumulate(summed, shard_index):
        offset = (shard_index * width).astype(jnp.int32)
        portion = lax.dynamic_slice_in_dim(three_centre, offset, width, 2).astype(jnp.float32)
        mask_part = lax.dynamic_slice_in_dim(block_mask, (shard_index * NB_DEV).astype(jnp.int32), NB_DEV, 2)
        screened = portion * expand_mask(mask_part, BS)
        columns = lax.dynamic_slice_in_dim(g_occ, offset, width, 0).astype(jnp.float32)
        return summed + jnp.einsum('pmn,ns->spm', screened, columns), None

    initial = jnp.zeros((NSIG, NP, NMU), jnp.float32)
    summed, unused = lax.scan(accumulate, initial, jnp.arange(N_COL, dtype=jnp.int32))
    occupied_half = summed.astype(jnp.bfloat16)
    result = jnp.einsum('spm,lm->spl', occupied_half.astype(jnp.float32), g_virt.astype(jnp.float32))
    return result.astype(jnp.bfloat16)
```

```python
import heapq

import jax
import jax.numpy as jnp
from jax import lax
from jax.experimental import pallas as pl
from jax.experimental.pallas import tpu as pltpu
from jax.sharding import PartitionSpec as P

MESH = pl.DeviceIdType.MESH
NZ, NX, NY = 12, 4, 8
NJ, NP, M, N, S = 4, 64, 128, 256, 192
F32, BF16 = jnp.float32, jnp.bfloat16

PIECES = [
    ("A", 12, "ring"),
    ("B", 12, "two"),
    ("A", 12, "ring"),
    ("B", 8, "two"),
    ("B", 12, "two"),
    ("B", 8, "two"),
]

PER_BYTE, LATENCY, PER_HOP = 2.0 / 91e3, 2.3, 0.45


def halves(n, flip):
    far, near = n // 2, (n - 1) // 2
    return (near, far) if flip else (far, near)


def plan(pieces):
    shapes, copies = {}, 0
    for i, (kind, width, way) in enumerate(pieces):
        rows = NJ * width
        if kind == "A":
            shapes[f"zpart{i}"] = pltpu.VMEM((NZ, NX * rows, M), F32)
            shapes[f"xpart{i}"] = pltpu.VMEM((NX, rows, M), F32)
            shapes[f"xsend{i}"] = pltpu.VMEM((NX, rows, M), BF16)
            shapes[f"xrecv{i}"] = pltpu.VMEM((NX - 1, rows, M), BF16)
            copies += NX - 1
        else:
            shapes[f"xpart{i}"] = pltpu.VMEM((NX, NZ * rows, M), F32)
            shapes[f"zpart{i}"] = pltpu.VMEM((NZ, rows, M), F32)
            for side, hops in enumerate(halves(NX, i % 2)):
                if hops:
                    shapes[f"xs{i}{side}"] = pltpu.VMEM((hops, NZ * rows, M), BF16)
                    shapes[f"xr{i}{side}"] = pltpu.VMEM((hops, NZ * rows, M), BF16)
            copies += NX - 1
        if way == "ring":
            zrows = rows * (NX if kind == "A" else 1)
            for side, hops in enumerate(halves(NZ, i % 2)):
                shapes[f"zs{i}{side}"] = pltpu.VMEM((hops, zrows, M), BF16)
                shapes[f"zr{i}{side}"] = pltpu.VMEM((hops, zrows, M), BF16)
            copies += NZ - 1
        else:
            shapes[f"zs{i}"] = pltpu.VMEM((3, NZ // 3, rows, M), BF16)
            shapes[f"zr{i}"] = pltpu.VMEM((2, NZ // 3, rows, M), BF16)
            shapes[f"zt{i}"] = pltpu.VMEM((NZ // 3, rows, M), BF16)
            shapes[f"zu{i}"] = pltpu.VMEM((3, rows, M), BF16)
            copies += 5
        shapes[f"gath{i}"] = pltpu.VMEM((2, NY, rows, M), BF16)
        copies += NY
    shapes["tc"] = pltpu.VMEM((NP, M, N), BF16)
    shapes["go"] = pltpu.VMEM((N, S), BF16)
    shapes["gv"] = pltpu.VMEM((M, 2 * NY * M), BF16)
    shapes["screen"] = pltpu.VMEM((M, N), BF16)
    shapes["gt"] = pltpu.VMEM((2, S, N), BF16)
    shapes["acc"] = pltpu.VMEM((NP * NJ, M), F32)
    shapes["load"] = pltpu.SemaphoreType.DMA((len(pieces) + 2,))
    shapes["sent"] = pltpu.SemaphoreType.DMA((copies,))
    shapes["came"] = pltpu.SemaphoreType.DMA((copies,))
    return shapes


def block_rows(rows):
    for size in (96, 80, 64, 48, 32, 16):
        if rows % size == 0:
            return size


def over_rows(rows, body):
    size = block_rows(rows)
    if rows == size:
        body(pl.ds(0, size))
    else:

        @pl.loop(0, rows // size)
        def _(b):
            body(pl.ds(pl.multiple_of(b * size, size), size))


class Builder:
    def __init__(self, pieces, refs):
        self.pieces, self.refs = pieces, refs
        self.now, self.free, self.handles, self.order, self.heap = 0.0, {}, [], 0, []
        row, col = lax.axis_index("row"), lax.axis_index("col")
        self.y, self.k = row // 2, lax.rem(row, 2)
        self.z, self.x = col // NX, lax.rem(col, NX)

    def at(self, axis, step):
        z, x, y, k = self.z, self.x, self.y, self.k
        if axis == "z":
            z = lax.rem(z + (step + NZ), NZ)
        elif axis == "x":
            x = lax.rem(x + (step + NX), NX)
        elif axis == "y":
            y = lax.rem(y + (step + NY), NY)
        else:
            k = 1 - k
        return (y * 2 + k, z * NX + x)

    def send(self, src, dst, axis, step):
        n = len(self.handles)
        copy = pltpu.make_async_remote_copy(
            src_ref=src,
            dst_ref=dst,
            send_sem=self.refs["sent"].at[n],
            recv_sem=self.refs["came"].at[n],
            device_id=self.at(axis, step),
            device_id_type=MESH,
        )
        copy.start()
        self.handles.append(copy)
        size = 2.0
        for length in src.shape:
            size *= length
        if axis == "k":
            return copy, self.now + 0.8 + size / 400e3
        ring = {"z": NZ, "x": NX, "y": NY}[axis]
        ahead = step % ring
        hops = min(ahead, ring - ahead)
        link = axis + ("+" if ahead * 2 <= ring else "-")
        begin = max(self.now, self.free.get(link, 0.0))
        self.free[link] = begin + hops * size * PER_BYTE
        self.now += 0.05
        return copy, begin + size * PER_BYTE * max(1, hops / 2) + LATENCY + PER_HOP * (hops - 1)

    def work(self, rows):
        self.now += 0.1 + rows / 8 * 0.004

    def push(self, ready, task):
        self.order += 1
        heapq.heappush(self.heap, (ready, self.order, task))

    def run(self):
        while self.heap:
            ready, _, task = heapq.heappop(self.heap)
            self.now = max(self.now, ready)
            for later in task:
                self.push(later, task)
                break

    def chain(self, part, send, recv, axis, ring, hops, sign, arrived):
        me = {"z": self.z, "x": self.x}[axis]
        rows = part.shape[1]
        for t in range(hops):
            owner = lax.rem(me + (sign * (hops - t) + ring), ring)
            if t:
                yield when
                copy.wait_recv()

            def body(block, t=t, owner=owner):
                value = part[owner, block]
                if t:
                    value = value + recv[t - 1, block].astype(F32)
                send[t, block] = value.astype(BF16)

            over_rows(rows, body)
            self.work(rows)
            copy, when = self.send(send.at[t], recv.at[t], axis, sign)
        arrived.append((copy, when, recv.at[hops - 1]))

    def both(self, i, part, name, axis, ring, then):
        arrived = []
        sides = [(side, hops) for side, hops in enumerate(halves(ring, i % 2)) if hops]

        def follow(task):
            yield from task
            if len(arrived) == len(sides):
                self.push(max(a[1] for a in arrived), then(arrived))

        for side, hops in sides:
            send, recv = self.refs[f"{name[0]}s{i}{side}"], self.refs[f"{name[0]}r{i}{side}"]
            task = self.chain(part, send, recv, axis, ring, hops, 1 - 2 * side, arrived)
            self.push(self.now, follow(task))

    def piece(self, i, first):
        kind, width, way = self.pieces[i]
        refs = self.refs
        rows = NJ * width
        refs_tc, screen = refs["tc"], refs["screen"]
        self.loads[i].wait()
        gt = refs["gt"].at[0 if kind == "A" else 1]
        into = refs[f"zpart{i}"] if kind == "A" else refs[f"xpart{i}"]
        blocks = NZ if kind == "A" else NX
        depth = S // blocks

        @pl.loop(0, width // 2)
        def _(q):
            tensor = (refs_tc[pl.ds(first + 2 * q, 2)] * screen[...][None]).reshape(2 * M, N)
            term = lax.dot_general(gt[...], tensor, (((1,), (1,)), ((), ())), preferred_element_type=F32)
            for u in range(2):
                at = pl.ds(pl.multiple_of((2 * q + u) * depth, depth), depth)
                into[:, at, :] = term[:, u * M : (u + 1) * M].reshape(blocks, depth, M)

        self.now += 0.05 * width
        if i == 0:
            pl.semaphore_wait(pltpu.get_barrier_semaphore(), self.peers)
        if kind == "A":
            self.both(i, into, "z", "z", NZ, lambda arrived: self.a_middle(i, first, arrived))
        else:
            self.both(i, into, "x", "x", NX, lambda arrived: self.b_middle(i, first, arrived))
        return
        yield

    def packed(self, value0, value1):
        upper = lax.broadcasted_iota(jnp.int32, value0.shape, 1) < NJ
        low = jnp.where(upper, value0, pltpu.roll(value1, NJ, 1))
        high = jnp.where(upper, pltpu.roll(value0, NJ, 1), value1)
        return low, high

    def repack(self, width, depth, part, owner, arrived, into, also=None):
        groups = depth // 8
        received = [a[2] for a in arrived]

        @pl.loop(0, width // 2)
        def _(q):
            at = pl.ds(pl.multiple_of(q * 2 * depth, 2 * depth), 2 * depth)
            value = part[owner, at]
            for ref in received:
                value = value + ref[at].astype(F32)
            value = value.reshape(2, groups, 8, M)
            low, high = self.packed(value[0], value[1])
            to = pl.ds(pl.multiple_of(q * 8, 8), 8)
            for g in range(groups):
                into[2 * g, to] = low[g]
                into[2 * g + 1, to] = high[g]

    def a_middle(self, i, first, arrived):
        kind, width, way = self.pieces[i]
        rows = NJ * width
        refs = self.refs
        for copy, _, _ in arrived:
            copy.wait_recv()
        xpart, xsend, xrecv = refs[f"xpart{i}"], refs[f"xsend{i}"], refs[f"xrecv{i}"]
        self.repack(width, NX * NJ, refs[f"zpart{i}"], self.z, arrived, xpart)
        xsend[...] = xpart[...].astype(BF16)
        self.work(8 * rows)
        copies = []
        for d in (2, 1, 3):
            to = lax.rem(self.x + d, NX)
            copies.append(self.send(xsend.at[to], xrecv.at[d - 1], "x", d))
        yield max(c[1] for c in copies)
        for copy, _ in copies:
            copy.wait_recv()
        value = xpart[self.x]
        for d in range(NX - 1):
            value = value + xrecv[d].astype(F32)
        yield from self.last(i, first, value)

    def b_middle(self, i, first, arrived):
        kind, width, way = self.pieces[i]
        rows = NJ * width
        refs = self.refs
        for copy, _, _ in arrived:
            copy.wait_recv()
        zpart = refs[f"zpart{i}"]
        self.repack(width, NZ * NJ, refs[f"xpart{i}"], self.x, arrived, zpart)
        self.work(24 * rows)
        if way == "ring":
            self.both(i, zpart, "z", "z", NZ, lambda came: self.b_end(i, first, came))
            return
        zs, zr, zt, zu = (refs[f"{name}{i}"] for name in ("zs", "zr", "zt", "zu"))
        for r in range(3):
            for c in range(NZ // 3):
                zs[r, c] = zpart[3 * c + r].astype(BF16)
        self.work(12 * rows)
        copies = []
        for side, step in enumerate((1, -1)):
            r = lax.rem(self.z + step + NZ, 3)
            copies.append(self.send(zs.at[r], zr.at[side], "z", step))
        yield max(c[1] for c in copies)
        for copy, _ in copies:
            copy.wait_recv()
        mine, home = lax.rem(self.z, 3), self.z // 3
        for c in range(NZ // 3):
            value = zpart[3 * c + mine] + zr[0, c].astype(F32) + zr[1, c].astype(F32)
            zpart[3 * c + mine] = value
            zt[c] = value.astype(BF16)
        self.work(8 * rows)
        copies = []
        for d in (2, 1, 3):
            to = lax.rem(home + d, NZ // 3)
            copies.append(self.send(zt.at[to], zu.at[d - 1], "z", 3 * d))
        yield max(c[1] for c in copies)
        for copy, _ in copies:
            copy.wait_recv()
        value = zpart[self.z]
        for d in range(3):
            value = value + zu[d].astype(F32)
        yield from self.last(i, first, value)

    def b_end(self, i, first, arrived):
        for copy, _, _ in arrived:
            copy.wait_recv()
        value = self.refs[f"zpart{i}"][self.z]
        for _, _, ref in arrived:
            value = value + ref[...].astype(F32)
        yield from self.last(i, first, value)

    def last(self, i, first, value):
        kind, width, way = self.pieces[i]
        rows = NJ * width
        gath = self.refs[f"gath{i}"]
        gath[self.k, self.y] = value.astype(BF16)
        self.work(3 * rows)
        own = gath.at[self.k, self.y]
        copies = [self.send(own, own, "y", d) for d in (4, 3, 5, 2, 6, 1, 7)]
        yield max(c[1] for c in copies)
        for copy, _ in copies:
            copy.wait_recv()
        half = gath.at[self.k]
        copy, when = self.send(half, half, "k", 1)
        yield when
        copy.wait_recv()
        gv = self.refs["gv"]
        total = jnp.zeros((rows, M), F32)
        for y in range(NY):
            left = jnp.concatenate([gath[0, y], gath[1, y]], axis=1)
            right = gv[:, 2 * M * y : 2 * M * (y + 1)]
            total += lax.dot_general(left, right, (((1,), (1,)), ((), ())), preferred_element_type=F32)
        self.refs["acc"][pl.ds(NJ * first, rows)] = total
        self.now += 0.4


def kernel(pieces, names, tensor, mask, occ, virt, out, *scratch):
    refs = dict(zip(names, scratch))
    b = Builder(pieces, refs)
    barrier = pltpu.get_barrier_semaphore()
    reached = [("z", d) for d in (1, -1)] + [("x", d) for d in (1, 2, 3)]
    if any(kind == "B" and way == "two" for kind, _, way in pieces):
        reached += [("z", d) for d in (3, 6, 9)]
    reached += [("y", d) for d in range(1, NY)] + [("k", 1)]
    for axis, step in reached:
        pl.semaphore_signal(barrier, inc=1, device_id=b.at(axis, step), device_id_type=MESH)
    b.peers = len(reached)
    load = refs["load"]
    occ_load = pltpu.make_async_copy(occ, refs["go"], load.at[len(pieces)])
    occ_load.start()
    b.loads, firsts, first = [], [], 0
    for i, (_, width, _) in enumerate(pieces):
        at = pl.ds(first, width)
        b.loads.append(pltpu.make_async_copy(tensor.at[at], refs["tc"].at[at], load.at[i]))
        b.loads[-1].start()
        firsts.append(first)
        first += width
    virt_load = pltpu.make_async_copy(virt, refs["gv"], load.at[len(pieces) + 1])
    virt_load.start()

    down = lax.broadcasted_iota(jnp.int32, (M, N), 0)
    along = lax.broadcasted_iota(jnp.int32, (M, N), 1)
    screen = jnp.zeros((M, N), F32)
    for mb in range(M // 64):
        for nb in range(N // 64):
            inside = (down // 64 == mb) & (along // 64 == nb)
            screen = jnp.where(inside, mask[0, mb, nb].astype(F32), screen)
    refs["screen"][...] = screen.astype(BF16)

    occ_load.wait()
    q = lax.broadcasted_iota(jnp.int32, (S, S), 0)
    s = lax.broadcasted_iota(jnp.int32, (S, S), 1)
    strip = NZ * NJ
    x = sum((q >= strip * c).astype(jnp.int32) for c in range(1, NX))
    rest = q - strip * x
    there = (rest >> 2) * (NX * NJ) + x * NJ + (rest & 3)
    for which, column in enumerate((q, there)):
        pick = (s == column).astype(F32).astype(BF16)
        turned = lax.dot_general(pick, refs["go"][...], (((1,), (1,)), ((), ())), preferred_element_type=F32)
        refs["gt"][which] = turned.astype(BF16)

    for i in range(len(pieces)):
        b.push(0.0, b.piece(i, firsts[i]))
    virt_load.wait()
    b.run()
    for copy in b.handles:
        copy.wait_send()
    for j in range(NJ):
        out[j] = refs["acc"][pl.ds(j, NP, stride=NJ), :].astype(BF16)


def shards(three_centre, block_mask, g_occ, g_virt):
    shapes = plan(PIECES)
    names = tuple(shapes)

    def body(*refs):
        kernel(PIECES, names, *refs)

    return pl.pallas_call(
        body,
        out_shape=jax.ShapeDtypeStruct((NJ, NP, M), BF16),
        in_specs=[
            pl.BlockSpec(memory_space=pl.ANY),
            pl.BlockSpec(memory_space=pltpu.SMEM),
            pl.BlockSpec(memory_space=pl.ANY),
            pl.BlockSpec(memory_space=pl.ANY),
        ],
        out_specs=pl.BlockSpec(memory_space=pltpu.VMEM),
        scratch_shapes=list(shapes.values()),
        compiler_params=pltpu.CompilerParams(
            collective_id=0, has_side_effects=True, vmem_limit_bytes=48 * 1024 * 1024
        ),
    )(three_centre, block_mask, g_occ, g_virt)


def solution(mesh):
    placed = (P(None, "row", "col"), P(None, "row", "col"), P("col", None), P("row", None))
    return jax.shard_map(
        shards, mesh=mesh, in_specs=placed, out_specs=P("col", None, "row"), check_vma=False
    )
```

```python
import heapq

import jax
import jax.numpy as jnp
from jax import lax
from jax.experimental import pallas as pl
from jax.experimental.pallas import tpu as pltpu
from jax.sharding import PartitionSpec as P

UNROLL = (4, 3, 2, 1)
MESH = pl.DeviceIdType.MESH
NZ, NX, NY = 12, 4, 8
NJ, NP, M, N, S = 4, 64, 128, 256, 192
F32, BF16 = jnp.float32, jnp.bfloat16

PIECES = [
    ("A", 16, "ring", "direct", "half", 0, 0, 4.3),
    ("B", 12, "two", "direct", "half", 1, 0, 5.8),
    ("B", 12, "two", "ring", "direct", 1, 1, 9.7),
    ("B", 8, "two", "ring", "direct", 0, 1, 13.8),
    ("A", 16, "ring", "direct", "half", 0, 0, 0.0),
]

PER_BYTE, LATENCY, PER_HOP = 2.0 / 97e3, 1.76, 0.45
PER_RI, PER_SEND, PER_STEP, PER_TILE = 0.077, 0.13, 0.11, 0.005


def halves(n, flip):
    far, near = n // 2, (n - 1) // 2
    return (near, far) if flip else (far, near)


def plan(pieces):
    shapes, copies = {}, 0
    for i, (kind, width, way, xway, yway, zflip, xflip, _) in enumerate(pieces):
        rows = NJ * width
        if kind == "A":
            shapes[f"zpart{i}"] = pltpu.VMEM((NZ, NX * rows, M), F32)
            shapes[f"xpart{i}"] = pltpu.VMEM((NX, rows, M), F32)
            shapes[f"xsend{i}"] = pltpu.VMEM((NX, rows, M), BF16)
            shapes[f"xrecv{i}"] = pltpu.VMEM((NX - 1, rows, M), BF16)
            copies += NX - 1
        else:
            shapes[f"xpart{i}"] = pltpu.VMEM((NX, NZ * rows, M), F32)
            shapes[f"zpart{i}"] = pltpu.VMEM((NZ, rows, M), F32)
            if xway == "ring":
                for side, hops in enumerate(halves(NX, xflip)):
                    shapes[f"xs{i}{side}"] = pltpu.VMEM((hops, NZ * rows, M), BF16)
                    shapes[f"xr{i}{side}"] = pltpu.VMEM((hops, NZ * rows, M), BF16)
            else:
                shapes[f"xsend{i}"] = pltpu.VMEM((NX, NZ * rows, M), BF16)
                shapes[f"xrecv{i}"] = pltpu.VMEM((NX - 1, NZ * rows, M), BF16)
            copies += NX - 1
        if way == "ring":
            zrows = rows * (NX if kind == "A" else 1)
            for side, hops in enumerate(halves(NZ, zflip)):
                shapes[f"zs{i}{side}"] = pltpu.VMEM((hops, zrows, M), BF16)
                shapes[f"zr{i}{side}"] = pltpu.VMEM((hops, zrows, M), BF16)
            copies += NZ - 1
        else:
            shapes[f"zs{i}"] = pltpu.VMEM((3, NZ // 3, rows, M), BF16)
            shapes[f"zr{i}"] = pltpu.VMEM((2, NZ // 3, rows, M), BF16)
            shapes[f"zt{i}"] = pltpu.VMEM((NZ // 3, rows, M), BF16)
            shapes[f"zu{i}"] = pltpu.VMEM((3, rows, M), BF16)
            copies += 5
        shapes[f"gath{i}"] = pltpu.VMEM((2, NY, rows, M), BF16)
        copies += NY if yway == "direct" else 6
    shapes["tc"] = pltpu.VMEM((NP, M, N), BF16)
    shapes["flags"] = pltpu.SMEM((1, M // 64, N // 64), jnp.int32)
    shapes["gv"] = pltpu.VMEM((M, 2 * NY * M), BF16)
    shapes["screen"] = pltpu.VMEM((M, N), BF16)
    shapes["gt"] = pltpu.VMEM((2, S, N), BF16)
    shapes["acc"] = pltpu.VMEM((NP * NJ, M), F32)
    shapes["load"] = pltpu.SemaphoreType.DMA((len(pieces) + 3,))
    shapes["sent"] = pltpu.SemaphoreType.DMA((copies,))
    shapes["came"] = pltpu.SemaphoreType.DMA((copies,))
    return shapes


def block_rows(rows):
    for size in (256, 240, 224, 208, 192, 176, 160, 144, 128, 112, 96, 80, 64, 48, 32, 16):
        if rows % size == 0:
            return size


def unrolled(count):
    return next(size for size in UNROLL if count % size == 0)


def over_rows(rows, body):
    size = block_rows(rows)
    if rows == size:
        body(pl.ds(0, size))
    else:

        @pl.loop(0, rows // size)
        def _(b):
            body(pl.ds(pl.multiple_of(b * size, size), size))


class Builder:
    def __init__(self, pieces, refs):
        self.pieces, self.refs = pieces, refs
        self.greeted = False
        self.now, self.free, self.handles, self.order, self.heap = 2.5, {}, [], 0, []
        row, col = lax.axis_index("row"), lax.axis_index("col")
        self.y, self.k = row // 2, lax.rem(row, 2)
        self.z, self.x = col // NX, lax.rem(col, NX)

    def at(self, axis, step):
        z, x, y, k = self.z, self.x, self.y, self.k
        if axis == "z":
            z = lax.rem(z + (step + NZ), NZ)
        elif axis == "x":
            x = lax.rem(x + (step + NX), NX)
        elif axis == "y":
            y = lax.rem(y + (step + NY), NY)
        else:
            k = 1 - k
        return (y * 2 + k, z * NX + x)

    def send(self, src, dst, axis, step):
        n = len(self.handles)
        copy = pltpu.make_async_remote_copy(
            src_ref=src,
            dst_ref=dst,
            send_sem=self.refs["sent"].at[n],
            recv_sem=self.refs["came"].at[n],
            device_id=self.at(axis, step),
            device_id_type=MESH,
        )
        copy.start()
        self.handles.append(copy)
        size = 2.0
        for length in src.shape:
            size *= length
        self.now += PER_SEND
        if axis == "k":
            return copy, self.now + 0.8 + size / 400e3
        ring = {"z": NZ, "x": NX, "y": NY}[axis]
        ahead = step % ring
        hops = min(ahead, ring - ahead)
        link = axis + ("+" if ahead * 2 <= ring else "-")
        begin = self.now
        for one, part in ((axis + "+", 0.5), (axis + "-", 0.5)) if ahead * 2 == ring else ((link, 1.0),):
            free = max(self.now, self.free.get(one, 0.0))
            self.free[one] = free + part * hops * size * PER_BYTE
            begin = max(begin, free)
        return copy, begin + size * PER_BYTE * max(1, hops / 2) + LATENCY + PER_HOP * (hops - 1)

    def work(self, rows):
        self.now += PER_STEP + rows / 8 * PER_TILE

    def push(self, ready, task):
        self.order += 1
        heapq.heappush(self.heap, (ready, self.order, task))

    def run(self):
        while self.heap:
            ready, _, task = heapq.heappop(self.heap)
            self.now = max(self.now, ready)
            for later in task:
                self.push(later, task)
                break

    def chain(self, part, send, recv, axis, ring, hops, sign, arrived):
        me = {"z": self.z, "x": self.x}[axis]
        rows = part.shape[1]
        for t in range(hops):
            owner = lax.rem(me + (sign * (hops - t) + ring), ring)
            if t:
                yield when
                copy.wait_recv()

            def body(block, t=t, owner=owner):
                value = part[owner, block]
                if t:
                    value = value + recv[t - 1, block].astype(F32)
                send[t, block] = value.astype(BF16)

            over_rows(rows, body)
            self.work(rows)
            copy, when = self.send(send.at[t], recv.at[t], axis, sign)
        arrived.append((copy, when, recv.at[hops - 1]))

    def both(self, i, part, axis, ring, flip, then):
        arrived = []
        sides = list(enumerate(halves(ring, flip)))

        def follow(task):
            yield from task
            if len(arrived) == len(sides):
                self.push(max(a[1] for a in arrived), then(arrived))

        for side, hops in sides:
            send, recv = self.refs[f"{axis}s{i}{side}"], self.refs[f"{axis}r{i}{side}"]
            task = self.chain(part, send, recv, axis, ring, hops, 1 - 2 * side, arrived)
            self.push(self.now, follow(task))

    def piece(self, i, first):
        kind, width, way, xway, yway, zflip, xflip, _ = self.pieces[i]
        refs = self.refs
        rows = NJ * width
        refs_tc, screen = refs["tc"], refs["screen"]
        self.loads[i].wait()
        gt = refs["gt"].at[0 if kind == "A" else 1]
        into = refs[f"zpart{i}"] if kind == "A" else refs[f"xpart{i}"]
        blocks = NZ if kind == "A" else NX
        depth = S // blocks

        @pl.loop(0, width // 2, unroll=unrolled(width // 2))
        def _(q):
            tensor = (refs_tc[pl.ds(first + 2 * q, 2)] * screen[...][None]).reshape(2 * M, N)
            term = lax.dot_general(gt[...], tensor, (((1,), (1,)), ((), ())), preferred_element_type=F32)
            for u in range(2):
                at = pl.ds(pl.multiple_of((2 * q + u) * depth, depth), depth)
                into[:, at, :] = term[:, u * M : (u + 1) * M].reshape(blocks, depth, M)

        self.now += PER_RI * width
        if not self.handles and not self.greeted:
            self.greeted = True
            pl.semaphore_wait(pltpu.get_barrier_semaphore(), self.peers)
        if kind == "A":
            self.both(i, into, "z", NZ, zflip, lambda arrived: self.a_middle(i, first, arrived))
        elif xway == "ring":
            self.both(i, into, "x", NX, xflip, lambda arrived: self.b_middle(i, first, arrived))
        else:
            send, recv = refs[f"xsend{i}"], refs[f"xrecv{i}"]
            arrived = []
            for d in (2, 1, 3):
                to = lax.rem(self.x + d, NX)

                def body(block, to=to):
                    send[to, block] = into[to, block].astype(BF16)

                over_rows(NZ * NJ * width, body)
                self.work(NZ * NJ * width)
                copy, when = self.send(send.at[to], recv.at[d - 1], "x", d)
                arrived.append((copy, when, recv.at[d - 1]))
            self.push(max(a[1] for a in arrived), self.b_middle(i, first, arrived))
        return
        yield

    def packed(self, value0, value1):
        upper = lax.broadcasted_iota(jnp.int32, value0.shape, 1) < NJ
        low = jnp.where(upper, value0, pltpu.roll(value1, NJ, 1))
        high = jnp.where(upper, pltpu.roll(value0, NJ, 1), value1)
        return low, high

    def repack(self, width, depth, part, owner, arrived, into, also=None):
        groups = depth // 8
        received = [a[2] for a in arrived]

        @pl.loop(0, width // 2, unroll=unrolled(width // 2))
        def _(q):
            at = pl.ds(pl.multiple_of(q * 2 * depth, 2 * depth), 2 * depth)
            value = part[owner, at]
            for ref in received:
                value = value + ref[at].astype(F32)
            value = value.reshape(2, groups, 8, M)
            low, high = self.packed(value[0], value[1])
            to = pl.ds(pl.multiple_of(q * 8, 8), 8)
            for g in range(groups):
                into[2 * g, to] = low[g]
                into[2 * g + 1, to] = high[g]

    def a_middle(self, i, first, arrived):
        kind, width, way, xway, yway, zflip, xflip, _ = self.pieces[i]
        rows = NJ * width
        refs = self.refs
        for copy, _, _ in arrived:
            copy.wait_recv()
        xpart, xsend, xrecv = refs[f"xpart{i}"], refs[f"xsend{i}"], refs[f"xrecv{i}"]
        self.repack(width, NX * NJ, refs[f"zpart{i}"], self.z, arrived, xpart)
        xsend[...] = xpart[...].astype(BF16)
        self.work(8 * rows)
        copies = []
        for d in (2, 1, 3):
            to = lax.rem(self.x + d, NX)
            copies.append(self.send(xsend.at[to], xrecv.at[d - 1], "x", d))
        yield max(c[1] for c in copies)
        for copy, _ in copies:
            copy.wait_recv()
        value = xpart[self.x]
        for d in range(NX - 1):
            value = value + xrecv[d].astype(F32)
        yield from self.last(i, first, value)

    def b_middle(self, i, first, arrived):
        kind, width, way, xway, yway, zflip, xflip, _ = self.pieces[i]
        rows = NJ * width
        refs = self.refs
        for copy, _, _ in arrived:
            copy.wait_recv()
        zpart = refs[f"zpart{i}"]
        self.repack(width, NZ * NJ, refs[f"xpart{i}"], self.x, arrived, zpart)
        self.work(24 * rows)
        if way == "ring":
            self.both(i, zpart, "z", NZ, zflip, lambda came: self.b_end(i, first, came))
            return
        zs, zr, zt, zu = (refs[f"{name}{i}"] for name in ("zs", "zr", "zt", "zu"))
        for r in range(3):
            for c in range(NZ // 3):
                zs[r, c] = zpart[3 * c + r].astype(BF16)
        self.work(12 * rows)
        copies = []
        for side, step in enumerate((1, -1)):
            r = lax.rem(self.z + step + NZ, 3)
            copies.append(self.send(zs.at[r], zr.at[side], "z", step))
        yield max(c[1] for c in copies)
        for copy, _ in copies:
            copy.wait_recv()
        mine, home = lax.rem(self.z, 3), self.z // 3
        for c in range(NZ // 3):
            value = zpart[3 * c + mine] + zr[0, c].astype(F32) + zr[1, c].astype(F32)
            zpart[3 * c + mine] = value
            zt[c] = value.astype(BF16)
        self.work(8 * rows)
        copies = []
        for d in (2, 1, 3):
            to = lax.rem(home + d, NZ // 3)
            copies.append(self.send(zt.at[to], zu.at[d - 1], "z", 3 * d))
        yield max(c[1] for c in copies)
        for copy, _ in copies:
            copy.wait_recv()
        value = zpart[self.z]
        for d in range(3):
            value = value + zu[d].astype(F32)
        yield from self.last(i, first, value)

    def b_end(self, i, first, arrived):
        for copy, _, _ in arrived:
            copy.wait_recv()
        value = self.refs[f"zpart{i}"][self.z]
        for _, _, ref in arrived:
            value = value + ref[...].astype(F32)
        yield from self.last(i, first, value)

    def last(self, i, first, value):
        kind, width, way, xway, yway, zflip, xflip, _ = self.pieces[i]
        rows = NJ * width
        gath = self.refs[f"gath{i}"]
        home = lax.rem(self.y, 2) * 4 + lax.rem(self.y // 2, 2) * 2 + self.y // 4
        gath[self.k, home] = value.astype(BF16)
        self.work(3 * rows)
        own = gath.at[self.k, home]
        steps = (4, 2, 6) if yway == "half" else (4, 3, 5, 2, 6, 1, 7)
        copies = [self.send(own, own, "y", d) for d in steps]
        yield max(c[1] for c in copies)
        for copy, _ in copies:
            copy.wait_recv()
        if yway == "half":
            copies = []
            for side, step in enumerate((1, -1)):
                both = gath.at[self.k, pl.ds(lax.rem(self.y, 2) * 4 + 2 * side, 2)]
                copies.append(self.send(both, both, "y", step))
            yield max(c[1] for c in copies)
            for copy, _ in copies:
                copy.wait_recv()
        half = gath.at[self.k]
        copy, when = self.send(half, half, "k", 1)
        yield when
        copy.wait_recv()
        gv = self.refs["gv"]
        total = jnp.zeros((rows, M), F32)
        for slot in range(NY):
            y = slot // 4 + 2 * (slot // 2 % 2) + 4 * (slot % 2)
            left = jnp.concatenate([gath[0, slot], gath[1, slot]], axis=1)
            right = gv[:, 2 * M * y : 2 * M * (y + 1)]
            total += lax.dot_general(left, right, (((1,), (1,)), ((), ())), preferred_element_type=F32)
        self.refs["acc"][pl.ds(NJ * first, rows)] = total
        self.now += 0.4


def kernel(pieces, names, tensor, mask, occ, virt, out, *scratch):
    refs = dict(zip(names, scratch))
    b = Builder(pieces, refs)
    barrier = pltpu.get_barrier_semaphore()
    reached = [("z", d) for d in (1, -1)] + [("x", d) for d in (1, 2, 3)]
    if any(kind == "B" and way == "two" for kind, _, way, *_ in pieces):
        reached += [("z", d) for d in (3, 6, 9)]
    reached += [("y", d) for d in range(1, NY)] + [("k", 1)]
    for axis, step in reached:
        pl.semaphore_signal(barrier, inc=1, device_id=b.at(axis, step), device_id_type=MESH)
    b.peers = len(reached)
    load = refs["load"]
    occ_load = pltpu.make_async_copy(occ, refs["gt"].at[0], load.at[len(pieces)])
    occ_load.start()
    mask_load = pltpu.make_async_copy(mask, refs["flags"], load.at[len(pieces) + 2])
    mask_load.start()
    b.loads, firsts, first = [], [], 0
    for i, (_, width, *_) in enumerate(pieces):
        at = pl.ds(first, width)
        b.loads.append(pltpu.make_async_copy(tensor.at[at], refs["tc"].at[at], load.at[i]))
        firsts.append(first)
        first += width
    for i in sorted(range(len(pieces)), key=lambda i: pieces[i][7]):
        b.loads[i].start()
    virt_load = pltpu.make_async_copy(virt, refs["gv"], load.at[len(pieces) + 1])
    virt_load.start()

    down = lax.broadcasted_iota(jnp.int32, (M, N), 0)
    along = lax.broadcasted_iota(jnp.int32, (M, N), 1)
    screen = jnp.zeros((M, N), F32)
    mask_load.wait()
    for mb in range(M // 64):
        for nb in range(N // 64):
            inside = (down // 64 == mb) & (along // 64 == nb)
            screen = jnp.where(inside, refs["flags"][0, mb, nb].astype(F32), screen)
    refs["screen"][...] = screen.astype(BF16)

    occ_load.wait()
    q = lax.broadcasted_iota(jnp.int32, (S, S), 0)
    s = lax.broadcasted_iota(jnp.int32, (S, S), 1)
    strip = NZ * NJ
    x = sum((q >= strip * c).astype(jnp.int32) for c in range(1, NX))
    rest = q - strip * x
    there = (rest >> 2) * (NX * NJ) + x * NJ + (rest & 3)
    pick = (s == there).astype(F32).astype(BF16)
    turned = lax.dot_general(pick, refs["gt"][0], (((1,), (0,)), ((), ())), preferred_element_type=F32)
    refs["gt"][1] = turned.astype(BF16)

    for i in range(len(pieces)):
        b.push(pieces[i][7], b.piece(i, firsts[i]))
    virt_load.wait()
    b.run()
    for copy in b.handles:
        copy.wait_send()
    for j in range(NJ):
        out[j] = refs["acc"][pl.ds(j, NP, stride=NJ), :].astype(BF16)


def shards(three_centre, block_mask, g_occ, g_virt):
    shapes = plan(PIECES)
    names = tuple(shapes)

    def body(*refs):
        kernel(PIECES, names, *refs)

    return pl.pallas_call(
        body,
        out_shape=jax.ShapeDtypeStruct((NJ, NP, M), BF16),
        in_specs=[
            pl.BlockSpec(memory_space=pltpu.HBM),
            pl.BlockSpec(memory_space=pltpu.HBM),
            pl.BlockSpec(memory_space=pltpu.HBM),
            pl.BlockSpec(memory_space=pltpu.HBM),
        ],
        out_specs=pl.BlockSpec(memory_space=pltpu.VMEM),
        scratch_shapes=list(shapes.values()),
        compiler_params=pltpu.CompilerParams(
            collective_id=0, has_side_effects=True, vmem_limit_bytes=48 * 1024 * 1024
        ),
    )(three_centre, block_mask, g_occ.T, g_virt)


def solution(mesh):
    placed = (P(None, "row", "col"), P(None, "row", "col"), P("col", None), P("row", None))
    return jax.shard_map(
        shards, mesh=mesh, in_specs=placed, out_specs=P("col", None, "row"), check_vma=False
    )
```

```python
import heapq

import jax
import jax.numpy as jnp
from jax import lax
from jax.experimental import pallas as pl
from jax.experimental.pallas import tpu as pltpu
from jax.sharding import PartitionSpec as P

UNROLL = (4, 3, 2, 1)
RETIRE = 10.0
MESH = pl.DeviceIdType.MESH
NZ, NX, NY = 12, 4, 8
NJ, NP, M, N, S = 4, 64, 128, 256, 192
F32, BF16 = jnp.float32, jnp.bfloat16

PIECES = [
    ("A", 12, "ring", "direct", "direct", 0, 0, 0.0),
    ("A", 12, "ring", "direct", "direct", 1, 0, 1.0),
    ("B", 12, "two", "ring", "direct", 1, 1, 0.0),
    ("B", 12, "two", "ring", "direct", 0, 0, 4.0),
    ("B", 16, "two", "ring", "direct", 0, 0, 8.0),
]

PER_BYTE, LATENCY, PER_HOP = 2.0 / 97e3, 1.76, 0.45
PER_RI, PER_SEND, PER_STEP, PER_TILE = 0.03, 0.13, 0.11, 0.004


def halves(n, flip):
    far, near = n // 2, (n - 1) // 2
    return (near, far) if flip else (far, near)


def plan(pieces):
    shapes, copies = {}, 0
    for i, (kind, width, way, xway, yway, zflip, xflip, _) in enumerate(pieces):
        rows = NJ * width
        if kind == "A":
            shapes[f"zpart{i}"] = pltpu.VMEM((NZ, NX * rows, M), F32)
            shapes[f"xpart{i}"] = pltpu.VMEM((NX, rows, M), F32)
            shapes[f"xsend{i}"] = pltpu.VMEM((NX, rows, M), BF16)
            shapes[f"xrecv{i}"] = pltpu.VMEM((NX - 1, rows, M), BF16)
            copies += NX - 1
        else:
            shapes[f"xpart{i}"] = pltpu.VMEM((NX, NZ * rows, M), F32)
            shapes[f"zpart{i}"] = pltpu.VMEM((NZ, rows, M), F32)
            if xway == "ring":
                for side, hops in enumerate(halves(NX, xflip)):
                    shapes[f"xs{i}{side}"] = pltpu.VMEM((hops, NZ * rows, M), BF16)
                    shapes[f"xr{i}{side}"] = pltpu.VMEM((hops, NZ * rows, M), BF16)
            else:
                shapes[f"xsend{i}"] = pltpu.VMEM((NX, NZ * rows, M), BF16)
                shapes[f"xrecv{i}"] = pltpu.VMEM((NX - 1, NZ * rows, M), BF16)
            copies += NX - 1
        if way == "ring":
            zrows = rows * (NX if kind == "A" else 1)
            for side, hops in enumerate(halves(NZ, zflip)):
                shapes[f"zs{i}{side}"] = pltpu.VMEM((hops, zrows, M), BF16)
                shapes[f"zr{i}{side}"] = pltpu.VMEM((hops, zrows, M), BF16)
            copies += NZ - 1
        elif way == "skip":
            zrows = rows * (NX if kind == "A" else 1)
            for side in range(2):
                shapes[f"zs{i}{side}"] = pltpu.VMEM((6, zrows, M), BF16)
                shapes[f"zr{i}{side}"] = pltpu.VMEM((6, zrows, M), BF16)
            copies += 7
        else:
            shapes[f"zs{i}"] = pltpu.VMEM((3, NZ // 3, rows, M), BF16)
            shapes[f"zr{i}"] = pltpu.VMEM((2, NZ // 3, rows, M), BF16)
            shapes[f"zt{i}"] = pltpu.VMEM((NZ // 3, rows, M), BF16)
            shapes[f"zu{i}"] = pltpu.VMEM((3, rows, M), BF16)
            copies += 5
        shapes[f"gath{i}"] = pltpu.VMEM((2, NY, rows, M), BF16)
        copies += NY if yway == "direct" else 6
    shapes["tc"] = pltpu.VMEM((NP, M, N), BF16)
    shapes["flags"] = pltpu.SMEM((1, M // 64, N // 64), jnp.int32)
    shapes["gv"] = pltpu.VMEM((M, 2 * NY * M), BF16)
    shapes["screen"] = pltpu.VMEM((M, N), BF16)
    shapes["gt"] = pltpu.VMEM((2, S, N), BF16)
    shapes["acc"] = pltpu.VMEM((NP * NJ, M), F32)
    shapes["load"] = pltpu.SemaphoreType.DMA((len(pieces) + 3,))
    shapes["sent"] = pltpu.SemaphoreType.DMA((copies,))
    shapes["came"] = pltpu.SemaphoreType.DMA((copies,))
    return shapes


def block_rows(rows):
    for size in (256, 240, 224, 208, 192, 176, 160, 144, 128, 112, 96, 80, 64, 48, 32, 16):
        if rows % size == 0:
            return size


def unrolled(count):
    return next(size for size in UNROLL if count % size == 0)


def over_rows(rows, body):
    size = block_rows(rows)
    if rows == size:
        body(pl.ds(0, size))
    else:

        @pl.loop(0, rows // size)
        def _(b):
            body(pl.ds(pl.multiple_of(b * size, size), size))


class Builder:
    def __init__(self, pieces, refs):
        self.pieces, self.refs = pieces, refs
        self.greeted, self.retired = False, 0
        self.now, self.free, self.handles, self.order, self.heap = 2.5, {}, [], 0, []
        row, col = lax.axis_index("row"), lax.axis_index("col")
        self.y, self.k = row // 2, lax.rem(row, 2)
        self.z, self.x = col // NX, lax.rem(col, NX)

    def at(self, axis, step):
        z, x, y, k = self.z, self.x, self.y, self.k
        if axis == "z":
            z = lax.rem(z + (step + NZ), NZ)
        elif axis == "x":
            x = lax.rem(x + (step + NX), NX)
        elif axis == "y":
            y = lax.rem(y + (step + NY), NY)
        else:
            k = 1 - k
        return (y * 2 + k, z * NX + x)

    def send(self, src, dst, axis, step):
        n = len(self.handles)
        copy = pltpu.make_async_remote_copy(
            src_ref=src,
            dst_ref=dst,
            send_sem=self.refs["sent"].at[n],
            recv_sem=self.refs["came"].at[n],
            device_id=self.at(axis, step),
            device_id_type=MESH,
        )
        copy.start()
        self.handles.append((copy, self.now))
        size = 2.0
        for length in src.shape:
            size *= length
        self.now += PER_SEND
        if axis == "k":
            return copy, self.now + 0.8 + size / 400e3
        ring = {"z": NZ, "x": NX, "y": NY}[axis]
        ahead = step % ring
        hops = min(ahead, ring - ahead)
        link = axis + ("+" if ahead * 2 <= ring else "-")
        begin = self.now
        for one, part in ((axis + "+", 0.5), (axis + "-", 0.5)) if ahead * 2 == ring else ((link, 1.0),):
            free = max(self.now, self.free.get(one, 0.0))
            self.free[one] = free + part * hops * size * PER_BYTE
            begin = max(begin, free)
        return copy, begin + size * PER_BYTE * max(1, hops / 2) + LATENCY + PER_HOP * (hops - 1)

    def work(self, rows):
        self.now += PER_STEP + rows / 8 * PER_TILE

    def push(self, ready, task):
        self.order += 1
        heapq.heappush(self.heap, (ready, self.order, task))

    def run(self):
        while self.heap:
            ready, _, task = heapq.heappop(self.heap)
            while self.now < ready and self.retired < len(self.handles):
                copy, sent = self.handles[self.retired]
                if sent + RETIRE > self.now:
                    break
                copy.wait_send()
                self.retired += 1
            self.now = max(self.now, ready)
            for later in task:
                self.push(later, task)
                break

    def chain(self, part, send, recv, axis, ring, hops, sign, arrived):
        me = {"z": self.z, "x": self.x}[axis]
        rows = part.shape[1]
        for t in range(hops):
            owner = lax.rem(me + (sign * (hops - t) + ring), ring)
            if t:
                yield when
                copy.wait_recv()

            def body(block, t=t, owner=owner):
                value = part[owner, block]
                if t:
                    value = value + recv[t - 1, block].astype(F32)
                send[t, block] = value.astype(BF16)

            over_rows(rows, body)
            self.work(rows)
            copy, when = self.send(send.at[t], recv.at[t], axis, sign)
        arrived.append((copy, when, recv.at[hops - 1]))

    def both(self, i, part, axis, ring, flip, then):
        arrived = []
        sides = list(enumerate(halves(ring, flip)))

        def follow(task):
            yield from task
            if len(arrived) == len(sides):
                self.push(max(a[1] for a in arrived), then(arrived))

        for side, hops in sides:
            send, recv = self.refs[f"{axis}s{i}{side}"], self.refs[f"{axis}r{i}{side}"]
            task = self.chain(part, send, recv, axis, ring, hops, 1 - 2 * side, arrived)
            self.push(self.now, follow(task))

    def stride(self, part, send, recv, far, sign, arrived):
        rows = part.shape[1]
        for t, ahead in enumerate((5, 3, 1)):
            owner = lax.rem(self.z + (sign * ahead + NZ), NZ)

            def body(block, t=t, owner=owner):
                send[t, block] = part[owner, block].astype(BF16)

            over_rows(rows, body)
        self.work(3 * rows)
        raw, when = self.send(send.at[pl.ds(0, 3)], recv.at[pl.ds(0, 3)], "z", sign)
        copy = None
        for t, ahead in enumerate((6, 4, 2)):
            if t == 0 and not far:
                continue
            if t:
                yield when
                if t == 1:
                    raw.wait_recv()
                if copy is not None:
                    copy.wait_recv()
            owner = lax.rem(self.z + (sign * ahead + NZ), NZ)
            before = t > 1 or (t == 1 and far)

            def body(block, t=t, owner=owner, before=before):
                value = part[owner, block]
                if t:
                    value = value + recv[t - 1, block].astype(F32)
                if before:
                    value = value + recv[t + 2, block].astype(F32)
                send[t + 3, block] = value.astype(BF16)

            over_rows(rows, body)
            self.work(1.5 * rows)
            copy, later = self.send(send.at[t + 3], recv.at[t + 3], "z", 2 * sign)
            when = later if t else max(when, later)
        arrived.append((copy, when, recv.at[5]))
        arrived.append((None, when, recv.at[2]))

    def strides(self, i, part, flip, then):
        arrived = []

        def follow(task):
            yield from task
            if len(arrived) == 4:
                self.push(max(a[1] for a in arrived), then(arrived))

        for side in range(2):
            send, recv = self.refs[f"zs{i}{side}"], self.refs[f"zr{i}{side}"]
            task = self.stride(part, send, recv, side == flip, 1 - 2 * side, arrived)
            self.push(self.now, follow(task))

    def piece(self, i, first):
        kind, width, way, xway, yway, zflip, xflip, _ = self.pieces[i]
        refs = self.refs
        rows = NJ * width
        refs_tc, screen = refs["tc"], refs["screen"]
        self.loads[i].wait()
        for copy in self.later:
            copy.start()
        self.later = []
        gt = refs["gt"].at[0 if kind == "A" else 1]
        into = refs[f"zpart{i}"] if kind == "A" else refs[f"xpart{i}"]
        blocks = NZ if kind == "A" else NX
        depth = S // blocks

        @pl.loop(0, width // 2, unroll=unrolled(width // 2))
        def _(q):
            tensor = (refs_tc[pl.ds(first + 2 * q, 2)] * screen[...][None]).reshape(2 * M, N)
            term = lax.dot_general(gt[...], tensor, (((1,), (1,)), ((), ())), preferred_element_type=F32)
            for u in range(2):
                at = pl.ds(pl.multiple_of((2 * q + u) * depth, depth), depth)
                into[:, at, :] = term[:, u * M : (u + 1) * M].reshape(blocks, depth, M)

        self.now += PER_RI * width
        if not self.handles and not self.greeted:
            self.greeted = True
            pl.semaphore_wait(pltpu.get_barrier_semaphore(), self.peers)
        if kind == "A" and way == "skip":
            self.strides(i, into, zflip, lambda arrived: self.a_middle(i, first, arrived))
        elif kind == "A":
            self.both(i, into, "z", NZ, zflip, lambda arrived: self.a_middle(i, first, arrived))
        elif xway == "ring":
            self.both(i, into, "x", NX, xflip, lambda arrived: self.b_middle(i, first, arrived))
        else:
            send, recv = refs[f"xsend{i}"], refs[f"xrecv{i}"]
            arrived = []
            for d in (2, 1, 3):
                to = lax.rem(self.x + d, NX)

                def body(block, to=to):
                    send[to, block] = into[to, block].astype(BF16)

                over_rows(NZ * NJ * width, body)
                self.work(NZ * NJ * width)
                copy, when = self.send(send.at[to], recv.at[d - 1], "x", d)
                arrived.append((copy, when, recv.at[d - 1]))
            self.push(max(a[1] for a in arrived), self.b_middle(i, first, arrived))
        return
        yield

    def packed(self, value0, value1):
        upper = lax.broadcasted_iota(jnp.int32, value0.shape, 1) < NJ
        low = jnp.where(upper, value0, pltpu.roll(value1, NJ, 1))
        high = jnp.where(upper, pltpu.roll(value0, NJ, 1), value1)
        return low, high

    def repack(self, width, depth, part, owner, arrived, into, also=None):
        groups = depth // 8
        received = [a[2] for a in arrived]

        @pl.loop(0, width // 2, unroll=unrolled(width // 2))
        def _(q):
            at = pl.ds(pl.multiple_of(q * 2 * depth, 2 * depth), 2 * depth)
            value = part[owner, at]
            for ref in received:
                value = value + ref[at].astype(F32)
            value = value.reshape(2, groups, 8, M)
            low, high = self.packed(value[0], value[1])
            to = pl.ds(pl.multiple_of(q * 8, 8), 8)
            for g in range(groups):
                into[2 * g, to] = low[g]
                into[2 * g + 1, to] = high[g]

    def a_middle(self, i, first, arrived):
        kind, width, way, xway, yway, zflip, xflip, _ = self.pieces[i]
        rows = NJ * width
        refs = self.refs
        for copy, _, _ in arrived:
            if copy is not None:
                copy.wait_recv()
        xpart, xsend, xrecv = refs[f"xpart{i}"], refs[f"xsend{i}"], refs[f"xrecv{i}"]
        self.repack(width, NX * NJ, refs[f"zpart{i}"], self.z, arrived, xpart)
        xsend[...] = xpart[...].astype(BF16)
        self.work(8 * rows)
        copies = []
        for d in (2, 1, 3):
            to = lax.rem(self.x + d, NX)
            copies.append(self.send(xsend.at[to], xrecv.at[d - 1], "x", d))
        yield max(c[1] for c in copies)
        for copy, _ in copies:
            copy.wait_recv()
        value = xpart[self.x]
        for d in range(NX - 1):
            value = value + xrecv[d].astype(F32)
        yield from self.last(i, first, value)

    def b_middle(self, i, first, arrived):
        kind, width, way, xway, yway, zflip, xflip, _ = self.pieces[i]
        rows = NJ * width
        refs = self.refs
        for copy, _, _ in arrived:
            copy.wait_recv()
        zpart = refs[f"zpart{i}"]
        self.repack(width, NZ * NJ, refs[f"xpart{i}"], self.x, arrived, zpart)
        self.work(24 * rows)
        if way == "ring":
            self.both(i, zpart, "z", NZ, zflip, lambda came: self.b_end(i, first, came))
            return
        if way == "skip":
            self.strides(i, zpart, zflip, lambda came: self.b_end(i, first, came))
            return
        zs, zr, zt, zu = (refs[f"{name}{i}"] for name in ("zs", "zr", "zt", "zu"))
        for r in range(3):
            for c in range(NZ // 3):
                zs[r, c] = zpart[3 * c + r].astype(BF16)
        self.work(12 * rows)
        copies = []
        for side, step in enumerate((1, -1)):
            r = lax.rem(self.z + step + NZ, 3)
            copies.append(self.send(zs.at[r], zr.at[side], "z", step))
        yield max(c[1] for c in copies)
        for copy, _ in copies:
            copy.wait_recv()
        mine, home = lax.rem(self.z, 3), self.z // 3
        for c in range(NZ // 3):
            value = zpart[3 * c + mine] + zr[0, c].astype(F32) + zr[1, c].astype(F32)
            zpart[3 * c + mine] = value
            zt[c] = value.astype(BF16)
        self.work(8 * rows)
        copies = []
        for d in (2, 1, 3):
            to = lax.rem(home + d, NZ // 3)
            copies.append(self.send(zt.at[to], zu.at[d - 1], "z", 3 * d))
        yield max(c[1] for c in copies)
        for copy, _ in copies:
            copy.wait_recv()
        value = zpart[self.z]
        for d in range(3):
            value = value + zu[d].astype(F32)
        yield from self.last(i, first, value)

    def b_end(self, i, first, arrived):
        for copy, _, _ in arrived:
            if copy is not None:
                copy.wait_recv()
        value = self.refs[f"zpart{i}"][self.z]
        for _, _, ref in arrived:
            value = value + ref[...].astype(F32)
        yield from self.last(i, first, value)

    def last(self, i, first, value):
        kind, width, way, xway, yway, zflip, xflip, _ = self.pieces[i]
        rows = NJ * width
        gath = self.refs[f"gath{i}"]
        home = lax.rem(self.y, 2) * 4 + lax.rem(self.y // 2, 2) * 2 + self.y // 4
        gath[self.k, home] = value.astype(BF16)
        self.work(3 * rows)
        own = gath.at[self.k, home]
        steps = (4, 2, 6) if yway == "half" else (4, 3, 5, 2, 6, 1, 7)
        copies = [self.send(own, own, "y", d) for d in steps]
        yield max(c[1] for c in copies)
        for copy, _ in copies:
            copy.wait_recv()
        if yway == "half":
            copies = []
            for side, step in enumerate((1, -1)):
                both = gath.at[self.k, pl.ds(lax.rem(self.y, 2) * 4 + 2 * side, 2)]
                copies.append(self.send(both, both, "y", step))
            yield max(c[1] for c in copies)
            for copy, _ in copies:
                copy.wait_recv()
        half = gath.at[self.k]
        copy, when = self.send(half, half, "k", 1)
        yield when
        copy.wait_recv()
        gv = self.refs["gv"]
        if self.virt_load is not None:
            self.virt_load.wait()
            self.virt_load = None
        total = jnp.zeros((rows, M), F32)
        for slot in range(NY):
            y = slot // 4 + 2 * (slot // 2 % 2) + 4 * (slot % 2)
            left = jnp.concatenate([gath[0, slot], gath[1, slot]], axis=1)
            right = gv[:, 2 * M * y : 2 * M * (y + 1)]
            total += lax.dot_general(left, right, (((1,), (1,)), ((), ())), preferred_element_type=F32)
        self.refs["acc"][pl.ds(NJ * first, rows)] = total
        self.now += 0.4


def kernel(pieces, names, tensor, mask, occ, virt, out, *scratch):
    refs = dict(zip(names, scratch))
    b = Builder(pieces, refs)
    load = refs["load"]
    occ_load = pltpu.make_async_copy(occ, refs["gt"].at[0], load.at[len(pieces)])
    occ_load.start()
    mask_load = pltpu.make_async_copy(mask, refs["flags"], load.at[len(pieces) + 2])
    mask_load.start()
    b.loads, firsts, first = [], [], 0
    for i, (_, width, *_) in enumerate(pieces):
        at = pl.ds(first, width)
        b.loads.append(pltpu.make_async_copy(tensor.at[at], refs["tc"].at[at], load.at[i]))
        firsts.append(first)
        first += width
    order = sorted(range(len(pieces)), key=lambda i: pieces[i][7])
    for i in order[:2]:
        b.loads[i].start()
    b.virt_load = pltpu.make_async_copy(virt, refs["gv"], load.at[len(pieces) + 1])
    b.later = [b.loads[i] for i in order[2:]] + [b.virt_load]
    barrier = pltpu.get_barrier_semaphore()
    reached = [("z", d) for d in (1, -1)] + [("x", d) for d in (1, 2, 3)]
    if any(way == "skip" for _, _, way, *_ in pieces):
        reached += [("z", d) for d in (2, -2)]
    if any(kind == "B" and way == "two" for kind, _, way, *_ in pieces):
        reached += [("z", d) for d in (3, 6, 9)]
    reached += [("y", d) for d in range(1, NY)] + [("k", 1)]
    for axis, step in reached:
        pl.semaphore_signal(barrier, inc=1, device_id=b.at(axis, step), device_id_type=MESH)
    b.peers = len(reached)

    down = lax.broadcasted_iota(jnp.int32, (M, N), 0)
    along = lax.broadcasted_iota(jnp.int32, (M, N), 1)
    screen = jnp.zeros((M, N), F32)
    mask_load.wait()
    for mb in range(M // 64):
        for nb in range(N // 64):
            inside = (down // 64 == mb) & (along // 64 == nb)
            screen = jnp.where(inside, refs["flags"][0, mb, nb].astype(F32), screen)
    refs["screen"][...] = screen.astype(BF16)

    occ_load.wait()
    q = lax.broadcasted_iota(jnp.int32, (S, S), 0)
    s = lax.broadcasted_iota(jnp.int32, (S, S), 1)
    strip = NZ * NJ
    x = sum((q >= strip * c).astype(jnp.int32) for c in range(1, NX))
    rest = q - strip * x
    there = (rest >> 2) * (NX * NJ) + x * NJ + (rest & 3)
    pick = (s == there).astype(F32).astype(BF16)
    turned = lax.dot_general(pick, refs["gt"][0], (((1,), (0,)), ((), ())), preferred_element_type=F32)
    refs["gt"][1] = turned.astype(BF16)

    for i in range(len(pieces)):
        b.push(pieces[i][7], b.piece(i, firsts[i]))
    b.run()
    for copy, _ in b.handles[b.retired :]:
        copy.wait_send()
    for j in range(NJ):
        out[j] = refs["acc"][pl.ds(j, NP, stride=NJ), :].astype(BF16)


def shards(three_centre, block_mask, g_occ, g_virt):
    shapes = plan(PIECES)
    names = tuple(shapes)

    def body(*refs):
        kernel(PIECES, names, *refs)

    return pl.pallas_call(
        body,
        out_shape=jax.ShapeDtypeStruct((NJ, NP, M), BF16),
        in_specs=[
            pl.BlockSpec(memory_space=pltpu.HBM),
            pl.BlockSpec(memory_space=pltpu.HBM),
            pl.BlockSpec(memory_space=pltpu.HBM),
            pl.BlockSpec(memory_space=pltpu.HBM),
        ],
        out_specs=pl.BlockSpec(memory_space=pltpu.VMEM),
        scratch_shapes=list(shapes.values()),
        compiler_params=pltpu.CompilerParams(
            collective_id=0, has_side_effects=True, vmem_limit_bytes=60 * 1024 * 1024
        ),
    )(three_centre, block_mask, g_occ.T, g_virt)


def solution(mesh):
    placed = (P(None, "row", "col"), P(None, "row", "col"), P("col", None), P("row", None))
    return jax.shard_map(
        shards, mesh=mesh, in_specs=placed, out_specs=P("col", None, "row"), check_vma=False
    )
```
